256 devices in a mesh: layer: 8 (over z_hi, core), tok: 32 (over x, z_lo, y).
Axes of the slice: x: 4, y: 4, z: 8 (z_hi: 4, z_lo: 2; z = z_hi * 2 + z_lo), core: 2. Of those that a mesh axis runs over, the one named last changes fastest.
Arguments:
- train_act: bfloat16 [16, 65536, 256], P('layer', 'tok'), may hold values from -0.75 to 0.75
- train_grad: bfloat16 [16, 65536, 256], P('layer', 'tok'), may hold values from -0.75 to 0.75
- test_act: bfloat16 [16, 2048, 256], P('layer', 'tok'), may hold values from -0.75 to 0.75
- test_grad: bfloat16 [16, 2048, 256], P('layer', 'tok'), may hold values from -0.75 to 0.75
- segment_ids: int32 [2048], replicated, may hold values from 0 to 127, as said below
Outputs:
- scores: float32 [128, 65536], P('layer', 'tok')
The draws below stay inside these ranges and needn't reach their ends.
Inputs may be any that keep to these rules, and one draw needn't show every extreme that they name: `segment_ids`: each of the 128 queries has exactly 16 test tokens, placed anywhere among the 2048.
All inputs are finite; a program needn't handle non-finite values.
Results may differ from the reference program's by a relative error of at most 0.0029.
Values may be sent and summed in bfloat16 or wider, within the bound.
No kernel may reach another device: no remote copies, remote signals or barrier semaphores. Data moves between devices by JAX's collectives and lax.ppermute only.
A program may use at most 128 MiB of HBM per device.

```python
import jax
import jax.numpy as jnp
from jax import lax

P_SIZE = 256
Q = 128
QTOK = 16
S = 2048
L = 16
TOKENS = 65536


def draw_segment_ids(key, part):
    order = jax.random.permutation(jax.random.fold_in(key, 7), S)
    return (order // QTOK).astype(jnp.int32)


def steps_of(own_key, dims, cuts, low, top_value):
    def one(position, blocks):
        heights = jax.random.uniform(jax.random.fold_in(jax.random.fold_in(own_key, 6), position), (blocks,), jnp.float32, low / len(cuts), top_value / len(cuts))
        return jnp.repeat(jnp.exp(heights), dims[position] // blocks).reshape((-1,) + (1,) * (len(dims) - position - 1))

    level = one(*cuts[0])
    for cut in cuts[1:]:
        level = level * one(*cut)
    return level


def bell_draw(key, shape, deviation, reach, pieces=(), kind=jnp.bfloat16):
    values = jax.random.normal(key, shape, jnp.float32) * deviation
    if len(pieces) > 0:
        values = steps_of(key, shape, pieces, -0.22, 0.18) * values
    return jnp.clip(values, min=-reach, max=reach).astype(kind)


def setup_inputs(seed: int = 0) -> dict:
    keys = jax.random.split(jax.random.key(seed), 6)
    return {
        "train_act": bell_draw(keys[0], (L, TOKENS, P_SIZE), 0.125, 0.75, ((0, 8), (1, 32))),
        "train_grad": bell_draw(keys[1], (L, TOKENS, P_SIZE), 0.125, 0.75, ((0, 8), (1, 32))),
        "test_act": bell_draw(keys[2], (L, S, P_SIZE), 0.125, 0.75, ((0, 8), (1, 32))),
        "test_grad": bell_draw(keys[3], (L, S, P_SIZE), 0.125, 0.75, ((0, 8), (1, 32))),
        "segment_ids": draw_segment_ids(jax.random.fold_in(keys[5], 71), 0),
    }


def reference(train_act, train_grad, test_act, test_grad, segment_ids):
    labels = jnp.arange(Q, dtype=jnp.int32)[:, None]
    select = (segment_ids[None, :] == labels).astype(jnp.bfloat16)

    def one_layer(running, tensors):
        act_train, grad_train, act_test, grad_test = tensors
        act_gram = jnp.einsum("sp,tp->st", act_test.astype(jnp.float32), act_train.astype(jnp.float32))
        grad_gram = jnp.einsum("sp,tp->st", grad_test.astype(jnp.float32), grad_train.astype(jnp.float32))
        product = (act_gram * grad_gram).astype(jnp.bfloat16)
        return running + jnp.dot(select, product, preferred_element_type=jnp.float32), None

    initial = jnp.zeros((Q, train_act.shape[1]), jnp.float32)
    scores, _ = lax.scan(one_layer, initial, (train_act, train_grad, test_act, test_grad))
    return scores
```

```python
import functools

import jax
import jax.numpy as jnp
from jax import lax
from jax.experimental import pallas as pl
from jax.experimental.pallas import tpu as pltpu
from jax.sharding import PartitionSpec as P

Q = 128
NX, NZ, NY = 4, 2, 4
OFFSETS = (0, -1, 1, 2)
BF16 = jnp.bfloat16
F32 = jnp.float32


def tok_moves(dx, dz, dy):
    moves = []
    for x in range(NX):
        for z in range(NZ):
            for y in range(NY):
                there = ((x + dx) % NX) * NZ * NY + ((z + dz) % NZ) * NY + (y + dy) % NY
                moves.append((x * NZ * NY + z * NY + y, there))
    return moves


def ring_gather(pair, forward, back):
    a, g = pair
    a_prev = lax.ppermute(a, "tok", forward)
    g_next = lax.ppermute(g, "tok", back)
    a_next = lax.ppermute(a, "tok", back)
    g_prev = lax.ppermute(g, "tok", forward)
    a_far = lax.ppermute(a_prev, "tok", forward)
    g_far = lax.ppermute(g_next, "tok", back)
    return [(a, g), (a_prev, g_prev), (a_next, g_next), (a_far, g_far)]


def chunk_kernel(last, n_pairs, ids_ref, labels_ref, ta_ref, tg_ref, *refs):
    tests = refs[: 2 * n_pairs]
    rest = refs[2 * n_pairs :]
    sel = (labels_ref[...] == ids_ref[0:1, :]).astype(F32).astype(BF16)
    if last:
        acc_ref, keep_ref, send_ref = rest
        acc = acc_ref[...]
    elif len(rest) == 2:
        acc_ref, out_ref = rest
        acc = acc_ref[...]
    else:
        (out_ref,) = rest
        acc = None
    nt = (((1,), (1,)), ((), ()))
    for layer in range(2):
        ta = ta_ref[layer]
        tg = tg_ref[layer]
        for n in range(n_pairs):
            a = tests[2 * n][:, layer].reshape(-1, 256)
            g = tests[2 * n + 1][:, layer].reshape(-1, 256)
            rows = a.shape[0]
            pa = lax.dot_general(a, ta, nt, preferred_element_type=F32)
            pg = lax.dot_general(g, tg, nt, preferred_element_type=F32)
            prod = (pa * pg).astype(BF16)
            part = jnp.dot(
                sel[:, n * rows : (n + 1) * rows], prod, preferred_element_type=F32
            )
            acc = part if acc is None else acc + part
    if last:
        keep_ref[...] = acc[: Q // 2]
        send_ref[...] = acc[Q // 2 :].astype(BF16)
    else:
        out_ref[...] = acc


def chunk(ids, labels, train_act, train_grad, pairs, acc, last):
    rows = train_act.shape[1]
    tile = 512
    steps = rows // tile
    tests = [t for pair in pairs for t in pair]
    whole = lambda a: pl.BlockSpec(a.shape, lambda i, nd=a.ndim: (0,) * nd)
    column = lambda n: pl.BlockSpec((n, tile), lambda i: (0, i))
    train = pl.BlockSpec((2, tile, 256), lambda i: (0, i, 0))
    args = [ids, labels, train_act, train_grad, *tests]
    in_specs = [whole(ids), whole(labels), train, train] + [whole(t) for t in tests]
    if acc is not None:
        args.append(acc)
        in_specs.append(column(Q))
    if last:
        out_shape = (
            jax.ShapeDtypeStruct((Q // 2, rows), F32),
            jax.ShapeDtypeStruct((Q // 2, rows), BF16),
        )
        out_specs = (column(Q // 2), column(Q // 2))
    else:
        out_shape = jax.ShapeDtypeStruct((Q, rows), F32)
        out_specs = column(Q)
    s_rows = sum(p[0].shape[0] * 64 for p in pairs)
    return pl.pallas_call(
        functools.partial(chunk_kernel, last, len(pairs)),
        grid=(steps,),
        in_specs=in_specs,
        out_specs=out_specs,
        out_shape=out_shape,
        compiler_params=pltpu.CompilerParams(vmem_limit_bytes=32 * 1024 * 1024),
        cost_estimate=pl.CostEstimate(
            flops=2 * 2 * s_rows * rows * (2 * 256 + Q),
            bytes_accessed=4 * 1024 * 1024 + 2 * Q * rows * 4,
            transcendentals=0,
        ),
    )(*args)


def merge_kernel(keep_ref, got_ref, own_ref, *send_refs):
    own_ref[...] = keep_ref[0:16] + got_ref[0:16].astype(F32)
    for k, ref in enumerate(send_refs, 1):
        rows = slice(16 * k, 16 * k + 16)
        ref[...] = (keep_ref[rows] + got_ref[rows].astype(F32)).astype(BF16)


def merge(keep, got):
    rows = keep.shape[1]
    send = jax.ShapeDtypeStruct((16, rows), BF16)
    return pl.pallas_call(
        merge_kernel,
        out_shape=(jax.ShapeDtypeStruct((16, rows), F32), send, send, send),
    )(keep, got)


def on_device(train_act, train_grad, test_act, test_grad, segment_ids):
    tok = lax.axis_index("tok")
    layer = lax.axis_index("layer")
    x, z, y = tok // 8, (tok // 4) % 2, tok % 4
    core, z_hi = layer % 2, layer // 2

    x_fwd, x_back = tok_moves(1, 0, 0), tok_moves(-1, 0, 0)
    y_fwd, y_back = tok_moves(0, 0, 1), tok_moves(0, 0, -1)
    across = tok_moves(0, 1, 0)

    ids = segment_ids.reshape(NX, NZ, NY, 64)
    ids = lax.dynamic_slice_in_dim(jnp.concatenate([ids, ids], 0), x, NX, 0)
    ids = lax.dynamic_slice_in_dim(jnp.concatenate([ids, ids], 1), z, NZ, 1)
    ids = lax.dynamic_slice_in_dim(jnp.concatenate([ids, ids], 2), y, NY, 2)
    order = [o % 4 for o in OFFSETS]
    reorder = lambda v, d: jnp.concatenate([lax.slice_in_dim(v, o, o + 1, axis=d) for o in order], d)
    ids = reorder(reorder(ids, 0), 2)
    first = ids[:, 0].reshape(4, 1, 256)
    second = jnp.swapaxes(ids[:, 1], 0, 1).reshape(4, 1, 256)
    chunk_ids = jnp.concatenate([first, second], 2)

    r = lax.broadcasted_iota(jnp.int32, (Q, 1), 0)
    labels = ((z_hi + (r % 64) // 16) % 4) * 32 + (core ^ (r // 64)) * 16 + r % 16

    own = (test_act, test_grad)
    other = tuple(lax.ppermute(t, "tok", across) for t in own)

    def stream(pair, first_dim, second_dim):
        near = ring_gather(pair, *first_dim)
        whole = tuple(jnp.stack([b[k] for b in near]) for k in range(2))
        return ring_gather(whole, *second_dim)

    one = stream(own, (y_fwd, y_back), (x_fwd, x_back))
    two = stream(other, (x_fwd, x_back), (y_fwd, y_back))

    acc = None
    for k in range(4):
        acc = chunk(
            chunk_ids[k], labels, train_act, train_grad, (one[k], two[k]), acc, k == 3
        )
    keep, send = acc

    swap = [(i, i ^ 1) for i in range(8)]
    got = lax.ppermute(send, "layer", swap)
    own_sum, *to_send = merge(keep, got)
    for k, part in enumerate(to_send, 1):
        moved = lax.ppermute(part, "layer", [(i, (i + 2 * k) % 8) for i in range(8)])
        own_sum = own_sum + moved.astype(F32)
    return own_sum


def solution(mesh):
    placed = (
        P("layer", "tok", None),
        P("layer", "tok", None),
        P("layer", "tok", None),
        P("layer", "tok", None),
        P(),
    )
    return jax.shard_map(
        on_device, mesh=mesh, in_specs=placed, out_specs=P("layer", "tok"), check_vma=False
    )
```

```python
import functools

import jax
import jax.numpy as jnp
from jax import lax
from jax.experimental import pallas as pl
from jax.experimental.pallas import tpu as pltpu
from jax.sharding import PartitionSpec as P

Q = 128
NX, NZ, NY = 4, 2, 4
NH, NC = 4, 2
ROWS = 32
BF16 = jnp.bfloat16
F32 = jnp.float32
AXES = ("layer", "tok")
SMALL = pltpu.CompilerParams(vmem_limit_bytes=4 * 1024 * 1024)
VMEM = pl.BlockSpec(memory_space=pltpu.VMEM)


def moves(step):
    pairs = []
    for h in range(NH):
        for c in range(NC):
            for x in range(NX):
                for z in range(NZ):
                    for y in range(NY):
                        to = step(h, c, x, z, y)
                        here, there = (
                            (((i[0] % NH * NC + i[1] % NC) * NX + i[2] % NX) * NZ + i[3] % NZ) * NY
                            + i[4] % NY
                            for i in ((h, c, x, z, y), to)
                        )
                        pairs.append((here, there))
    return pairs


def first_ring(d):
    return moves(lambda h, c, x, z, y: (h, c, x, z, y + d) if c == 0 else (h, c, x + d, z, y))


def second_ring(d):
    return moves(lambda h, c, x, z, y: (h, c, x + d, z, y) if c == 0 else (h, c, x, z, y + d))


def send(value, pairs):
    return lax.ppermute(value, AXES, pairs)


def pack_kernel(core_ref, a_ref, g_ref, sib_a_ref, sib_g_ref, out_ref):
    rows = pl.ds(pl.multiple_of(core_ref[0] * ROWS, ROWS), ROWS)
    for layer in range(2):
        for k, refs in enumerate(((a_ref, sib_a_ref), (g_ref, sib_g_ref))):
            out_ref[layer, k] = refs[0][layer, rows]
            out_ref[2 + layer, k] = refs[1][layer, rows]


def pack(core, a, g, sib_a, sib_g):
    return pl.pallas_call(
        pack_kernel,
        in_specs=[pl.BlockSpec(memory_space=pltpu.SMEM)] + [VMEM] * 4,
        out_specs=VMEM,
        out_shape=jax.ShapeDtypeStruct((4, 2, ROWS, 256), BF16),
        compiler_params=SMALL,
    )(core.reshape(1), a, g, sib_a, sib_g)


def chunk_kernel(last, has_acc, n_blocks, ids_ref, labels_ref, *refs):
    trains = refs[:4]
    blocks = refs[4 : 4 + n_blocks]
    rest = refs[4 + n_blocks :]
    acc_ref = rest[0] if has_acc else None
    outs = rest[1:] if has_acc else rest
    sel = (labels_ref[...] == ids_ref[0:1, :]).astype(F32).astype(BF16)
    nt = (((1,), (1,)), ((), ()))
    rows = trains[0].shape[1]
    tile = 1024
    width = 4 * ROWS
    for j in range(rows // tile):
        cols = slice(j * tile, (j + 1) * tile)
        prods, sels = [], []
        for layer in range(4):
            ta = trains[2 * (layer // 2)][layer % 2, cols]
            tg = trains[2 * (layer // 2) + 1][layer % 2, cols]
            a = jnp.concatenate([b[:, layer, 0].reshape(width, 256) for b in blocks], 0)
            g = jnp.concatenate([b[:, layer, 1].reshape(width, 256) for b in blocks], 0)
            pa = lax.dot_general(a, ta, nt, preferred_element_type=F32)
            pg = lax.dot_general(g, tg, nt, preferred_element_type=F32)
            prods.append((pa * pg).astype(BF16))
            sels.append(sel)
        part = jnp.dot(
            jnp.concatenate(sels, 1), jnp.concatenate(prods, 0), preferred_element_type=F32
        )
        if has_acc:
            part = part + acc_ref[:, cols]
        if last:
            outs[0][:, cols] = part[: Q // 2]
            outs[1][:, cols] = part[Q // 2 :].astype(BF16)
        else:
            outs[0][:, cols] = part


def chunk(ids, labels, trains, blocks, acc, last):
    rows = trains[0].shape[1]
    args = [ids, labels, *trains, *blocks]
    if acc is not None:
        args.append(acc)
    if last:
        out_shape = (
            jax.ShapeDtypeStruct((Q // 2, rows), F32),
            jax.ShapeDtypeStruct((Q // 2, rows), BF16),
        )
        out_specs = (VMEM, VMEM)
    else:
        out_shape = jax.ShapeDtypeStruct((Q, rows), F32)
        out_specs = VMEM
    s_rows = 4 * ROWS * len(blocks)
    return pl.pallas_call(
        functools.partial(chunk_kernel, last, acc is not None, len(blocks)),
        in_specs=[VMEM] * len(args),
        out_specs=out_specs,
        out_shape=out_shape,
        compiler_params=pltpu.CompilerParams(vmem_limit_bytes=24 * 1024 * 1024),
        cost_estimate=pl.CostEstimate(
            flops=2 * 4 * s_rows * rows * (2 * 256 + Q),
            bytes_accessed=1024 * 1024,
            transcendentals=0,
        ),
    )(*args)


def merge_kernel(keep_ref, got_ref, own_ref, *send_refs):
    own_ref[...] = keep_ref[0:16] + got_ref[0:16].astype(F32)
    for k, ref in enumerate(send_refs, 1):
        rows = slice(16 * k, 16 * k + 16)
        ref[...] = (keep_ref[rows] + got_ref[rows].astype(F32)).astype(BF16)


def merge(keep, got):
    rows = keep.shape[1]
    part = jax.ShapeDtypeStruct((16, rows), BF16)
    return pl.pallas_call(
        merge_kernel,
        in_specs=[VMEM] * 2,
        out_specs=(VMEM,) * 4,
        out_shape=(jax.ShapeDtypeStruct((16, rows), F32), part, part, part),
        compiler_params=SMALL,
    )(keep, got)


def total_kernel(own_ref, *refs):
    total = own_ref[...]
    for ref in refs[:-1]:
        total = total + ref[...].astype(F32)
    refs[-1][...] = total


def total(own, parts):
    return pl.pallas_call(
        total_kernel,
        in_specs=[VMEM] * 4,
        out_specs=VMEM,
        out_shape=jax.ShapeDtypeStruct(own.shape, F32),
        compiler_params=SMALL,
    )(own, *parts)


def chunk_queries(segment_ids, core, x, z, y):
    ids = segment_ids.reshape(NX, NZ, NY, 2, ROWS)
    ids = jnp.where(core == 0, ids[:, :, :, 0], ids[:, :, :, 1])
    turned = jnp.where(core == 0, ids, jnp.swapaxes(ids, 0, 2))
    second, first = jnp.where(core == 0, x, y), jnp.where(core == 0, y, x)
    both = jnp.concatenate([turned, turned], 0)
    ids = lax.dynamic_slice_in_dim(both, second, 4, 0)
    ids = lax.dynamic_slice_in_dim(jnp.concatenate([ids, ids], 1), z, 2, 1)
    ids = lax.dynamic_slice_in_dim(jnp.concatenate([ids, ids], 2), first, 4, 2)
    order = (0, 3, 1, 2)
    ids = jnp.concatenate([ids[o : o + 1] for o in order], 0)
    ids = jnp.concatenate([ids[:, :, o : o + 1] for o in order], 2)
    return ids.reshape(4, 1, 2 * 4 * ROWS)


def on_device(train_act, train_grad, test_act, test_grad, segment_ids):
    tok = lax.axis_index("tok")
    layer = lax.axis_index("layer")
    x, z, y = tok // 8, (tok // 4) % 2, tok % 4
    core, z_hi = layer % 2, layer // 2

    sibling = moves(lambda h, c, x, z, y: (h, 1 - c, x, z, y))
    partner = moves(lambda h, c, x, z, y: (h, c, x, 1 - z, y))

    sib_a = send(test_act, sibling)
    sib_g = send(test_grad, sibling)
    block = pack(core, test_act, test_grad, sib_a, sib_g)
    sib_ta = send(train_act, sibling)
    sib_tg = send(train_grad, sibling)
    trains = (train_act, train_grad, sib_ta, sib_tg)

    chunk_ids = chunk_queries(segment_ids, core, x, z, y)
    r = lax.broadcasted_iota(jnp.int32, (Q, 1), 0)
    labels = ((z_hi + (r % 64) // 16) % 4) * 32 + (core ^ (r // 64)) * 16 + r % 16

    other = send(block, partner)

    def near(value):
        return jnp.stack([value] + [send(value, first_ring(d)) for d in (1, -1, 2)])

    low, high = near(block), near(other)
    forward, back = second_ring(1), second_ring(-1)
    low_prev, low_next = send(low, forward), send(low, back)
    high_prev, high_next = send(high, forward), send(high, back)
    low_far, high_far = send(low_prev, forward), send(high_next, back)

    half = 4 * ROWS
    run = functools.partial(chunk, labels=labels, trains=trains)
    acc = run(ids=chunk_ids[0], blocks=(low, high), acc=None, last=False)
    acc = run(ids=chunk_ids[1], blocks=(low_prev, high_prev), acc=acc, last=False)
    acc = run(ids=chunk_ids[2], blocks=(low_next, high_next), acc=acc, last=False)
    acc = run(ids=chunk_ids[3][:, :half], blocks=(low_far,), acc=acc, last=False)
    keep, give = run(ids=chunk_ids[3][:, half:], blocks=(high_far,), acc=acc, last=True)

    got = send(give, sibling)
    own, *parts = merge(keep, got)
    parts = [
        send(part, moves(lambda h, c, x, z, y: (h + k, c, x, z, y)))
        for k, part in enumerate(parts, 1)
    ]
    return total(own, parts)


def solution(mesh):
    placed = (
        P("layer", "tok", None),
        P("layer", "tok", None),
        P("layer", "tok", None),
        P("layer", "tok", None),
        P(),
    )
    return jax.shard_map(
        on_device, mesh=mesh, in_specs=placed, out_specs=P("layer", "tok"), check_vma=False
    )
```

```python
import functools

import jax
import jax.numpy as jnp
from jax import lax
from jax.experimental import pallas as pl
from jax.experimental.pallas import tpu as pltpu
from jax.sharding import PartitionSpec as P

Q = 128
NX, NZ, NY = 4, 2, 4
NH, NC = 4, 2
BLOCK = 64
ORDER = (0, 3, 1, 2)
BF16 = jnp.bfloat16
F32 = jnp.float32
AXES = ("layer", "tok")
SMALL = pltpu.CompilerParams(vmem_limit_bytes=4 * 1024 * 1024)
SMEM = pl.BlockSpec(memory_space=pltpu.SMEM)
VMEM = pl.BlockSpec(memory_space=pltpu.VMEM)


def moves(step):
    pairs = []
    for h in range(NH):
        for c in range(NC):
            for x in range(NX):
                for z in range(NZ):
                    for y in range(NY):
                        to = step(h, c, x, z, y)
                        here, there = (
                            (((i[0] % NH * NC + i[1] % NC) * NX + i[2] % NX) * NZ + i[3] % NZ) * NY
                            + i[4] % NY
                            for i in ((h, c, x, z, y), to)
                        )
                        pairs.append((here, there))
    return pairs


def along_x(d):
    return moves(lambda h, c, x, z, y: (h, c, x + d, z, y))


def along_y(d):
    return moves(lambda h, c, x, z, y: (h, c, x, z, y + d))


def along_z(d):
    return moves(lambda h, c, x, z, y: (h + d, c, x, z, y))


def send(value, pairs):
    return lax.ppermute(value, AXES, pairs)


def prepare_kernel(layer_ref, tok_ref, ids_ref, query_ref, label_ref, turned):
    core, z_hi = layer_ref[0] % 2, layer_ref[0] // 2
    x, z, y = tok_ref[0] // 8, tok_ref[0] // 4 % 2, tok_ref[0] % 4
    ids = ids_ref[...]
    turned[0:16] = ids
    turned[16:32] = pltpu.roll(ids, 64, 1)
    lane = lax.broadcasted_iota(jnp.int32, (1, 128), 1)
    for row, far in enumerate(ORDER):
        for half in range(2):
            for pair in range(2):
                got = []
                for n in range(2):
                    near = ORDER[2 * pair + n]
                    p, q = (far, near) if half == 0 else (near, far)
                    tok = (x + p) % 4 * 8 + (z + half) % 2 * 4 + (y + q) % 4
                    turn = (tok + n) % 2
                    got.append(turned[pl.ds(turn * 16 + tok // 2, 1), :])
                at = 256 * half + 128 * pair
                query_ref[row : row + 1, at : at + 128] = jnp.where(lane < 64, got[0], got[1])
    r = lax.broadcasted_iota(jnp.int32, (Q, 1), 0)
    owner = jnp.where(r < 64, core, 1 - core)
    label_ref[...] = (z_hi + (r % 64) // 16) % 4 * 32 + owner * 16 + r % 16


def prepare(layer, tok, segment_ids):
    return pl.pallas_call(
        prepare_kernel,
        in_specs=[SMEM, SMEM, VMEM],
        out_specs=(VMEM, VMEM),
        out_shape=(
            jax.ShapeDtypeStruct((4, 2 * 4 * BLOCK), jnp.int32),
            jax.ShapeDtypeStruct((Q, 1), jnp.int32),
        ),
        scratch_shapes=[pltpu.VMEM((32, 128), jnp.int32)],
        compiler_params=SMALL,
    )(layer.reshape(1), tok.reshape(1), segment_ids.reshape(16, 128))


def chunk_kernel(pieces, first, last, n_blocks, ids_ref, labels_ref, ta_ref, tg_ref, *refs):
    blocks, rest = refs[:n_blocks], refs[n_blocks:]
    trains = (ta_ref, tg_ref)
    width = 4 * BLOCK
    tile = 1024
    ids = jnp.concatenate(
        [ids_ref[r : r + 1, width * h : width * h + width] for r, h in pieces], 1
    )
    sel = (labels_ref[...] == ids).astype(F32).astype(BF16)
    nt = (((1,), (1,)), ((), ()))
    outs = rest if first else rest[1:]
    for j in range(ta_ref.shape[1] // tile):
        cols = slice(j * tile, (j + 1) * tile)
        prods = []
        for layer in range(2):
            grams = []
            for k in range(2):
                test = jnp.concatenate([b[:, k, layer].reshape(width, 256) for b in blocks], 0)
                grams.append(
                    lax.dot_general(test, trains[k][layer, cols], nt, preferred_element_type=F32)
                )
            prods.append((grams[0] * grams[1]).astype(BF16))
        part = jnp.dot(
            jnp.concatenate([sel] * 2, 1), jnp.concatenate(prods, 0), preferred_element_type=F32
        )
        if not first:
            part = part + rest[0][:, cols]
        if last:
            outs[0][:, cols] = part[: Q // 2]
            outs[1][:, cols] = part[Q // 2 :].astype(BF16)
        else:
            outs[0][:, cols] = part


def chunk(pieces, blocks, acc, last, ids, labels, trains):
    first = acc is None
    rows = trains[0].shape[1]
    args = [ids, labels, *trains, *blocks] + ([] if first else [acc])
    if last:
        out_shape = (
            jax.ShapeDtypeStruct((Q // 2, rows), F32),
            jax.ShapeDtypeStruct((Q // 2, rows), BF16),
        )
    else:
        out_shape = jax.ShapeDtypeStruct((Q, rows), F32)
    s_rows = 4 * BLOCK * len(blocks)
    return pl.pallas_call(
        functools.partial(chunk_kernel, pieces, first, last, len(blocks)),
        in_specs=[VMEM] * len(args),
        out_specs=(VMEM, VMEM) if last else VMEM,
        out_shape=out_shape,
        compiler_params=pltpu.CompilerParams(vmem_limit_bytes=16 * 1024 * 1024),
        cost_estimate=pl.CostEstimate(
            flops=2 * 2 * s_rows * rows * (2 * 256 + Q),
            bytes_accessed=1024 * 1024,
            transcendentals=0,
        ),
    )(*args)


def merge_kernel(keep_ref, got_ref, own_ref, *send_refs):
    own_ref[...] = keep_ref[0:16] + got_ref[0:16].astype(F32)
    for k, ref in enumerate(send_refs, 1):
        rows = slice(16 * k, 16 * k + 16)
        ref[...] = (keep_ref[rows] + got_ref[rows].astype(F32)).astype(BF16)


def merge(keep, got):
    rows = keep.shape[1]
    part = jax.ShapeDtypeStruct((16, rows), BF16)
    return pl.pallas_call(
        merge_kernel,
        in_specs=[VMEM] * 2,
        out_specs=(VMEM,) * 4,
        out_shape=(jax.ShapeDtypeStruct((16, rows), F32), part, part, part),
        compiler_params=SMALL,
    )(keep, got)


def total_kernel(own_ref, *refs):
    total = own_ref[...]
    for ref in refs[:-1]:
        total = total + ref[...].astype(F32)
    refs[-1][...] = total


def total(own, parts):
    return pl.pallas_call(
        total_kernel,
        in_specs=[VMEM] * 4,
        out_specs=VMEM,
        out_shape=jax.ShapeDtypeStruct(own.shape, F32),
        compiler_params=SMALL,
    )(own, *parts)


def on_device(train_act, train_grad, test_act, test_grad, segment_ids):
    layer, tok = lax.axis_index("layer"), lax.axis_index("tok")
    sibling = moves(lambda h, c, x, z, y: (h, 1 - c, x, z, y))
    partner = moves(lambda h, c, x, z, y: (h, c, x, 1 - z, y))

    block = jnp.stack([test_act, test_grad])
    other = send(block, partner)
    ids, labels = prepare(layer, tok, segment_ids)
    low = jnp.stack([block] + [send(block, along_y(d)) for d in (1, -1, 2)])
    other, ids, labels = lax.optimization_barrier((other, ids, labels))
    high = jnp.stack([other] + [send(other, along_x(d)) for d in (1, -1, 2)])

    lows = [low] + [send(low, along_x(d)) for d in (1, -1, 2)]
    highs = [high] + [send(high, along_y(d)) for d in (1, -1, 2)]
    run = functools.partial(chunk, ids=ids, labels=labels, trains=(train_act, train_grad))
    acc = run(((0, 0),), lows[:1], None, False)
    acc = run(((0, 1),), highs[:1], acc, False)
    acc = run(((1, 0),), lows[1:2], acc, False)
    acc = run(((2, 0),), lows[2:3], acc, False)
    acc = run(((1, 1),), highs[1:2], acc, False)
    acc = run(((2, 1),), highs[2:3], acc, False)
    acc = run(((3, 0),), lows[3:], acc, False)
    keep, give = run(((3, 1),), highs[3:], acc, True)

    own, *parts = merge(keep, send(give, sibling))
    parts = [send(parts[k - 1], along_z(k)) for k in (2, 1, 3)]
    return total(own, parts)


def solution(mesh):
    placed = (
        P("layer", "tok", None),
        P("layer", "tok", None),
        P("layer", "tok", None),
        P("layer", "tok", None),
        P(),
    )
    return jax.shard_map(
        on_device, mesh=mesh, in_specs=placed, out_specs=P("layer", "tok"), check_vma=False
    )
```

```python
import functools

import jax
import jax.numpy as jnp
from jax import lax
from jax.experimental import pallas as pl
from jax.experimental.pallas import tpu as pltpu
from jax.sharding import PartitionSpec as P

Q = 128
NX, NZ, NY = 4, 2, 4
NH, NC = 4, 2
BLOCK = 64
ORDER = (0, 2, 3, 1)
BF16 = jnp.bfloat16
F32 = jnp.float32
AXES = ("layer", "tok")
SMALL = pltpu.CompilerParams(vmem_limit_bytes=4 * 1024 * 1024)
SMEM = pl.BlockSpec(memory_space=pltpu.SMEM)
VMEM = pl.BlockSpec(memory_space=pltpu.VMEM)


def moves(step):
    pairs = []
    for h in range(NH):
        for c in range(NC):
            for x in range(NX):
                for z in range(NZ):
                    for y in range(NY):
                        to = step(h, c, x, z, y)
                        here, there = (
                            (((i[0] % NH * NC + i[1] % NC) * NX + i[2] % NX) * NZ + i[3] % NZ) * NY
                            + i[4] % NY
                            for i in ((h, c, x, z, y), to)
                        )
                        pairs.append((here, there))
    return pairs


def along_x(d):
    return moves(lambda h, c, x, z, y: (h, c, x + d, z, y))


def along_y(d):
    return moves(lambda h, c, x, z, y: (h, c, x, z, y + d))


def along_z(d):
    return moves(lambda h, c, x, z, y: (h + d, c, x, z, y))


def send(value, pairs):
    return lax.ppermute(value, AXES, pairs)


def prepare_kernel(layer_ref, tok_ref, ids_ref, query_ref, label_ref, turned):
    core, z_hi = layer_ref[0] % 2, layer_ref[0] // 2
    x, z, y = tok_ref[0] // 8, tok_ref[0] // 4 % 2, tok_ref[0] % 4
    ids = ids_ref[...]
    turned[0:16] = ids
    turned[16:32] = pltpu.roll(ids, 64, 1)
    lane = lax.broadcasted_iota(jnp.int32, (1, 128), 1)
    for row, far in enumerate(ORDER):
        for half in range(2):
            for pair in range(2):
                got = []
                for n in range(2):
                    near = ORDER[2 * pair + n]
                    p, q = (far, near) if half == 0 else (near, far)
                    tok = (x + p) % 4 * 8 + (z + half) % 2 * 4 + (y + q) % 4
                    turn = (tok + n) % 2
                    got.append(turned[pl.ds(turn * 16 + tok // 2, 1), :])
                at = 256 * half + 128 * pair
                query_ref[row : row + 1, at : at + 128] = jnp.where(lane < 64, got[0], got[1])
    r = lax.broadcasted_iota(jnp.int32, (Q, 1), 0)
    owner = jnp.where(r < 64, core, 1 - core)
    label_ref[...] = (z_hi + (r % 64) // 16) % 4 * 32 + owner * 16 + r % 16


def prepare(layer, tok, segment_ids):
    return pl.pallas_call(
        prepare_kernel,
        in_specs=[SMEM, SMEM, VMEM],
        out_specs=(VMEM, VMEM),
        out_shape=(
            jax.ShapeDtypeStruct((4, 2 * 4 * BLOCK), jnp.int32),
            jax.ShapeDtypeStruct((Q, 1), jnp.int32),
        ),
        scratch_shapes=[pltpu.VMEM((32, 128), jnp.int32)],
        compiler_params=SMALL,
    )(layer.reshape(1), tok.reshape(1), segment_ids.reshape(16, 128))


def chunk_kernel(pieces, first, last, n_blocks, ids_ref, labels_ref, ta_ref, tg_ref, *refs):
    blocks, rest = refs[:n_blocks], refs[n_blocks:]
    trains = (ta_ref, tg_ref)
    width = 4 * BLOCK
    tile = 1024
    ids = jnp.concatenate(
        [ids_ref[r : r + 1, width * h : width * h + width] for r, h in pieces], 1
    )
    sel = (labels_ref[...] == ids).astype(F32).astype(BF16)
    nt = (((1,), (1,)), ((), ()))
    outs = rest if first else rest[1:]
    for j in range(ta_ref.shape[1] // tile):
        cols = slice(j * tile, (j + 1) * tile)
        prods = []
        for layer in range(2):
            grams = []
            for k in range(2):
                test = jnp.concatenate([b[:, k, layer].reshape(-1, 256) for b in blocks], 0)
                grams.append(
                    lax.dot_general(test, trains[k][layer, cols], nt, preferred_element_type=F32)
                )
            prods.append((grams[0] * grams[1]).astype(BF16))
        part = jnp.dot(
            jnp.concatenate([sel] * 2, 1), jnp.concatenate(prods, 0), preferred_element_type=F32
        )
        if not first:
            part = part + rest[0][:, cols]
        if last:
            outs[0][:, cols] = part[: Q // 2]
            outs[1][:, cols] = part[Q // 2 :].astype(BF16)
        else:
            outs[0][:, cols] = part


def chunk(pieces, blocks, acc, last, ids, labels, trains):
    first = acc is None
    rows = trains[0].shape[1]
    args = [ids, labels, *trains, *blocks] + ([] if first else [acc])
    if last:
        out_shape = (
            jax.ShapeDtypeStruct((Q // 2, rows), F32),
            jax.ShapeDtypeStruct((Q // 2, rows), BF16),
        )
    else:
        out_shape = jax.ShapeDtypeStruct((Q, rows), F32)
    s_rows = BLOCK * sum(b.shape[0] for b in blocks)
    return pl.pallas_call(
        functools.partial(chunk_kernel, pieces, first, last, len(blocks)),
        in_specs=[VMEM] * len(args),
        out_specs=(VMEM, VMEM) if last else VMEM,
        out_shape=out_shape,
        compiler_params=pltpu.CompilerParams(vmem_limit_bytes=16 * 1024 * 1024),
        cost_estimate=pl.CostEstimate(
            flops=2 * 2 * s_rows * rows * (2 * 256 + Q),
            bytes_accessed=1024 * 1024,
            transcendentals=0,
        ),
    )(*args)


def merge_kernel(keep_ref, got_ref, own_ref, *send_refs):
    own_ref[...] = keep_ref[0:16] + got_ref[0:16].astype(F32)
    for k, ref in enumerate(send_refs, 1):
        rows = slice(16 * k, 16 * k + 16)
        ref[...] = (keep_ref[rows] + got_ref[rows].astype(F32)).astype(BF16)


def merge(keep, got):
    rows = keep.shape[1]
    part = jax.ShapeDtypeStruct((16, rows), BF16)
    return pl.pallas_call(
        merge_kernel,
        in_specs=[VMEM] * 2,
        out_specs=(VMEM,) * 4,
        out_shape=(jax.ShapeDtypeStruct((16, rows), F32), part, part, part),
        compiler_params=SMALL,
    )(keep, got)


def total_kernel(own_ref, *refs):
    total = own_ref[...]
    for ref in refs[:-1]:
        total = total + ref[...].astype(F32)
    refs[-1][...] = total


def total(own, parts):
    return pl.pallas_call(
        total_kernel,
        in_specs=[VMEM] * 4,
        out_specs=VMEM,
        out_shape=jax.ShapeDtypeStruct(own.shape, F32),
        compiler_params=SMALL,
    )(own, *parts)


def on_device(train_act, train_grad, test_act, test_grad, segment_ids):
    layer, tok = lax.axis_index("layer"), lax.axis_index("tok")
    sibling = moves(lambda h, c, x, z, y: (h, 1 - c, x, z, y))
    partner = moves(lambda h, c, x, z, y: (h, c, x, 1 - z, y))

    block = jnp.stack([test_act, test_grad])
    other = send(block, partner)
    trains = (train_act, train_grad)
    ids, labels = prepare(layer, tok, segment_ids)
    low = jnp.stack([block] + [send(block, along_y(d)) for d in (2, 1, -1)])
    other, ids, labels = lax.optimization_barrier((other, ids, labels))
    run = functools.partial(chunk, ids=ids, labels=labels, trains=trains)
    acc = run(((0, 0),), (low,), None, False)
    ring = [send(other, along_x(d)) for d in (2, 1, -1)]
    ring, acc = lax.optimization_barrier((ring, acc))
    high = jnp.stack([other] + ring)

    low_prev, low_next = send(low, along_x(1)), send(low, along_x(-1))
    high_prev, high_next = send(high, along_y(1)), send(high, along_y(-1))
    low_far = (send(low_prev[:2], along_x(1)), send(low_next[2:], along_x(-1)))
    high_far = (send(high_prev[:2], along_y(1)), send(high_next[2:], along_y(-1)))
    acc = run(((0, 1),), (high,), acc, False)
    acc = run(((2, 0), (3, 0)), (low_prev, low_next), acc, False)
    high_prev, high_next, acc = lax.optimization_barrier((high_prev, high_next, acc))
    acc = run(((2, 1), (3, 1)), (high_prev, high_next), acc, False)
    acc = run(((1, 0),), low_far, acc, False)
    keep, give = run(((1, 1),), high_far, acc, True)

    own, *parts = merge(keep, send(give, sibling))
    parts = [send(parts[k - 1], along_z(k)) for k in (2, 1, 3)]
    return total(own, parts)


def solution(mesh):
    placed = (
        P("layer", "tok", None),
        P("layer", "tok", None),
        P("layer", "tok", None),
        P("layer", "tok", None),
        P(),
    )
    return jax.shard_map(
        on_device, mesh=mesh, in_specs=placed, out_specs=P("layer", "tok"), check_vma=False
    )
```

```python
import functools

import jax
import jax.numpy as jnp
from jax import lax
from jax.experimental import pallas as pl
from jax.experimental.pallas import tpu as pltpu
from jax.sharding import PartitionSpec as P

Q = 128
NX, NZ, NY = 4, 2, 4
NH, NC = 4, 2
BLOCK = 64
ORDER = (0, 2, 3, 1)
BF16 = jnp.bfloat16
F32 = jnp.float32
AXES = ("layer", "tok")
SMALL = pltpu.CompilerParams(vmem_limit_bytes=4 * 1024 * 1024)
HBM = pl.BlockSpec(memory_space=pltpu.HBM)
SMEM = pl.BlockSpec(memory_space=pltpu.SMEM)
VMEM = pl.BlockSpec(memory_space=pltpu.VMEM)


def moves(step):
    pairs = []
    for h in range(NH):
        for c in range(NC):
            for x in range(NX):
                for z in range(NZ):
                    for y in range(NY):
                        to = step(h, c, x, z, y)
                        here, there = (
                            (((i[0] % NH * NC + i[1] % NC) * NX + i[2] % NX) * NZ + i[3] % NZ) * NY
                            + i[4] % NY
                            for i in ((h, c, x, z, y), to)
                        )
                        pairs.append((here, there))
    return pairs


def one_way(d):
    return moves(lambda h, c, x, z, y: (h, c, x + d, z, y) if c == 0 else (h, c, x, z, y + d))


def other_way(d):
    return moves(lambda h, c, x, z, y: (h, c, x, z, y + d) if c == 0 else (h, c, x + d, z, y))


def along_z(d):
    return moves(lambda h, c, x, z, y: (h + d, c, x, z, y))


def send(value, pairs):
    return lax.ppermute(value, AXES, pairs)


def prepare_kernel(layer_ref, tok_ref, ids_ref, query_ref, label_ref, turned):
    core, z_hi = layer_ref[0] % 2, layer_ref[0] // 2
    x, z, y = tok_ref[0] // 8, tok_ref[0] // 4 % 2, tok_ref[0] % 4
    ids = ids_ref[...]
    turned[0:16] = ids
    turned[16:32] = pltpu.roll(ids, 64, 1)
    lane = lax.broadcasted_iota(jnp.int32, (1, 128), 1)
    for row, far in enumerate(ORDER):
        for half in range(2):
            for pair in range(2):
                got = []
                for n in range(2):
                    near = ORDER[2 * pair + n]
                    p, q = (far, near) if half == 0 else (near, far)
                    p, q = jnp.where(core == 0, p, q), jnp.where(core == 0, q, p)
                    tok = (x + p) % 4 * 8 + (z + half) % 2 * 4 + (y + q) % 4
                    turn = (tok + n) % 2
                    got.append(turned[pl.ds(turn * 16 + tok // 2, 1), :])
                at = 256 * half + 128 * pair
                query_ref[row : row + 1, at : at + 128] = jnp.where(lane < 64, got[0], got[1])
    r = lax.broadcasted_iota(jnp.int32, (Q, 1), 0)
    owner = jnp.where(r < 64, core, 1 - core)
    label_ref[...] = (z_hi + (r % 64) // 16) % 4 * 32 + owner * 16 + r % 16


def prepare(layer, tok, segment_ids):
    return pl.pallas_call(
        prepare_kernel,
        in_specs=[SMEM, SMEM, VMEM],
        out_specs=(VMEM, VMEM),
        out_shape=(
            jax.ShapeDtypeStruct((4, 2 * 4 * BLOCK), jnp.int32),
            jax.ShapeDtypeStruct((Q, 1), jnp.int32),
        ),
        scratch_shapes=[pltpu.VMEM((32, 128), jnp.int32)],
        compiler_params=SMALL,
    )(layer.reshape(1), tok.reshape(1), segment_ids.reshape(16, 128))


def chunk_kernel(pieces, first, last, n_blocks, ids_ref, labels_ref, ta_ref, tg_ref, *refs):
    blocks, rest = refs[:n_blocks], refs[n_blocks:]
    trains = (ta_ref, tg_ref)
    width = 4 * BLOCK
    tile = 1024
    ids = jnp.concatenate(
        [ids_ref[r : r + 1, width * h : width * h + width] for r, h in pieces], 1
    )
    sel = (labels_ref[...] == ids).astype(F32).astype(BF16)
    nt = (((1,), (1,)), ((), ()))
    outs = rest if first else rest[1:]
    tiles = ta_ref.shape[1] // tile
    copies = {}
    if first:
        kept, sems = rest[1:3], rest[3]
        for j in range(tiles):
            for layer in range(2):
                for k in range(2):
                    piece = (layer, slice(j * tile, (j + 1) * tile))
                    copies[j, layer, k] = pltpu.make_async_copy(
                        trains[k].at[piece], kept[k].at[piece], sems.at[j, layer, k]
                    )
        for copy in copies.values():
            copy.start()
        trains = kept
    for j in range(tiles):
        cols = slice(j * tile, (j + 1) * tile)
        prods = []
        for layer in range(2):
            grams = []
            for k in range(2):
                if first:
                    copies[j, layer, k].wait()
                test = jnp.concatenate([b[:, k, layer].reshape(-1, 256) for b in blocks], 0)
                grams.append(
                    lax.dot_general(test, trains[k][layer, cols], nt, preferred_element_type=F32)
                )
            prods.append((grams[0] * grams[1]).astype(BF16))
        part = jnp.dot(
            jnp.concatenate([sel] * 2, 1), jnp.concatenate(prods, 0), preferred_element_type=F32
        )
        if not first:
            part = part + rest[0][:, cols]
        if last:
            outs[0][:, cols] = part[: Q // 2]
            outs[1][:, cols] = part[Q // 2 :].astype(BF16)
        else:
            outs[0][:, cols] = part


def chunk(pieces, blocks, acc, last, ids, labels, trains):
    first = acc is None
    rows = trains[0].shape[1]
    args = [ids, labels, *trains, *blocks] + ([] if first else [acc])
    if last:
        out_shape = (
            jax.ShapeDtypeStruct((Q // 2, rows), F32),
            jax.ShapeDtypeStruct((Q // 2, rows), BF16),
        )
    else:
        out_shape = (jax.ShapeDtypeStruct((Q, rows), F32),)
    if first:
        out_shape += tuple(jax.ShapeDtypeStruct(t.shape, t.dtype) for t in trains)
    s_rows = BLOCK * sum(b.shape[0] for b in blocks)
    return pl.pallas_call(
        functools.partial(chunk_kernel, pieces, first, last, len(blocks)),
        in_specs=[VMEM] * 2 + [HBM if first else VMEM] * 2 + [VMEM] * (len(args) - 4),
        out_specs=(VMEM,) * len(out_shape),
        out_shape=out_shape,
        scratch_shapes=[pltpu.SemaphoreType.DMA((rows // 1024, 2, 2))] if first else [],
        compiler_params=pltpu.CompilerParams(vmem_limit_bytes=(48 if first else 16) * 1024 * 1024),
        cost_estimate=pl.CostEstimate(
            flops=2 * 2 * s_rows * rows * (2 * 256 + Q),
            bytes_accessed=1024 * 1024,
            transcendentals=0,
        ),
    )(*args)


def merge_kernel(keep_ref, got_ref, own_ref, *send_refs):
    own_ref[...] = keep_ref[0:16] + got_ref[0:16].astype(F32)
    for k, ref in enumerate(send_refs, 1):
        rows = slice(16 * k, 16 * k + 16)
        ref[...] = (keep_ref[rows] + got_ref[rows].astype(F32)).astype(BF16)


def merge(keep, got):
    rows = keep.shape[1]
    part = jax.ShapeDtypeStruct((16, rows), BF16)
    return pl.pallas_call(
        merge_kernel,
        in_specs=[VMEM] * 2,
        out_specs=(VMEM,) * 4,
        out_shape=(jax.ShapeDtypeStruct((16, rows), F32), part, part, part),
        compiler_params=SMALL,
    )(keep, got)


def total_kernel(own_ref, *refs):
    total = own_ref[...]
    for ref in refs[:-1]:
        total = total + ref[...].astype(F32)
    refs[-1][...] = total


def total(own, parts):
    return pl.pallas_call(
        total_kernel,
        in_specs=[VMEM] * 4,
        out_specs=VMEM,
        out_shape=jax.ShapeDtypeStruct(own.shape, F32),
        compiler_params=SMALL,
    )(own, *parts)


def on_device(train_act, train_grad, test_act, test_grad, segment_ids):
    layer, tok = lax.axis_index("layer"), lax.axis_index("tok")
    sibling = moves(lambda h, c, x, z, y: (h, 1 - c, x, z, y))
    partner = moves(lambda h, c, x, z, y: (h, c, x, 1 - z, y))

    block = jnp.stack([test_act, test_grad])
    other = send(block, partner)
    trains = (train_act, train_grad)
    ids, labels = prepare(layer, tok, segment_ids)
    low = jnp.stack([block] + [send(block, other_way(d)) for d in (2, 1, -1)])
    other, ids, labels = lax.optimization_barrier((other, ids, labels))
    run = functools.partial(chunk, ids=ids, labels=labels, trains=trains)
    acc, *trains = run(((0, 0),), (low,), None, False)
    run = functools.partial(chunk, ids=ids, labels=labels, trains=trains)
    ring = [send(other, one_way(d)) for d in (-1, 1, 2)]
    ring, acc = lax.optimization_barrier((ring, acc))
    high = jnp.stack([other] + ring[::-1])

    low_prev, low_next = send(low, one_way(1)), send(low, one_way(-1))
    high_prev, high_next = send(high, other_way(1)), send(high, other_way(-1))
    low_far = (send(low_prev[:2], one_way(1)), send(low_next[2:], one_way(-1)))
    high_far = (send(high_prev[:2], other_way(1)), send(high_next[2:], other_way(-1)))
    (acc,) = run(((0, 1),), (high,), acc, False)
    (acc,) = run(((2, 0), (3, 0)), (low_prev, low_next), acc, False)
    high_prev, high_next, acc = lax.optimization_barrier((high_prev, high_next, acc))
    (acc,) = run(((2, 1), (3, 1)), (high_prev, high_next), acc, False)
    (acc,) = run(((1, 0),), low_far, acc, False)
    keep, give = run(((1, 1),), high_far, acc, True)

    own, *parts = merge(keep, send(give, sibling))
    parts = [send(parts[k - 1], along_z(k)) for k in (2, 1, 3)]
    return total(own, parts)


def solution(mesh):
    placed = (
        P("layer", "tok", None),
        P("layer", "tok", None),
        P("layer", "tok", None),
        P("layer", "tok", None),
        P(),
    )
    return jax.shard_map(
        on_device, mesh=mesh, in_specs=placed, out_specs=P("layer", "tok"), check_vma=False
    )
```

```python
import functools

import jax
import jax.numpy as jnp
from jax import lax
from jax.experimental import pallas as pl
from jax.experimental.pallas import tpu as pltpu
from jax.sharding import PartitionSpec as P

Q = 128
NX, NZ, NY = 4, 2, 4
NH, NC = 4, 2
BLOCK = 64
ORDER = (0, 2, 3, 1)
BF16 = jnp.bfloat16
F32 = jnp.float32
AXES = ("layer", "tok")
SMALL = pltpu.CompilerParams(vmem_limit_bytes=4 * 1024 * 1024)
HBM = pl.BlockSpec(memory_space=pltpu.HBM)
SMEM = pl.BlockSpec(memory_space=pltpu.SMEM)
VMEM = pl.BlockSpec(memory_space=pltpu.VMEM)


def moves(step):
    pairs = []
    for h in range(NH):
        for c in range(NC):
            for x in range(NX):
                for z in range(NZ):
                    for y in range(NY):
                        to = step(h, c, x, z, y)
                        here, there = (
                            (((i[0] % NH * NC + i[1] % NC) * NX + i[2] % NX) * NZ + i[3] % NZ) * NY
                            + i[4] % NY
                            for i in ((h, c, x, z, y), to)
                        )
                        pairs.append((here, there))
    return pairs


def one_way(d):
    return moves(lambda h, c, x, z, y: (h, c, x + d, z, y) if c == 0 else (h, c, x, z, y + d))


def other_way(d):
    return moves(lambda h, c, x, z, y: (h, c, x, z, y + d) if c == 0 else (h, c, x + d, z, y))


def along_z(d):
    return moves(lambda h, c, x, z, y: (h + d if c == 0 else h - d, c, x, z, y))


def send(value, pairs):
    return lax.ppermute(value, AXES, pairs)


def prepare_kernel(layer_ref, tok_ref, ids_ref, query_ref, label_ref, turned):
    core, z_hi = layer_ref[0] % 2, layer_ref[0] // 2
    x, z, y = tok_ref[0] // 8, tok_ref[0] // 4 % 2, tok_ref[0] % 4
    ids = ids_ref[...]
    turned[0:16] = ids
    turned[16:32] = pltpu.roll(ids, 64, 1)
    lane = lax.broadcasted_iota(jnp.int32, (1, 128), 1)
    for row, far in enumerate(ORDER):
        for half in range(2):
            for pair in range(2):
                got = []
                for n in range(2):
                    near = ORDER[2 * pair + n]
                    p, q = (far, near) if half == 0 else (near, far)
                    p, q = jnp.where(core == 0, p, q), jnp.where(core == 0, q, p)
                    tok = (x + p) % 4 * 8 + (z + half) % 2 * 4 + (y + q) % 4
                    turn = (tok + n) % 2
                    got.append(turned[pl.ds(turn * 16 + tok // 2, 1), :])
                at = 256 * half + 128 * pair
                query_ref[row : row + 1, at : at + 128] = jnp.where(lane < 64, got[0], got[1])
    r = lax.broadcasted_iota(jnp.int32, (Q, 1), 0)
    owner = jnp.where(r < 64, core, 1 - core)
    part = (r % 64) // 16
    label_ref[...] = (z_hi + jnp.where(owner == 0, part, 4 - part)) % 4 * 32 + owner * 16 + r % 16


def prepare(layer, tok, segment_ids):
    return pl.pallas_call(
        prepare_kernel,
        in_specs=[SMEM, SMEM, VMEM],
        out_specs=(VMEM, VMEM),
        out_shape=(
            jax.ShapeDtypeStruct((4, 2 * 4 * BLOCK), jnp.int32),
            jax.ShapeDtypeStruct((Q, 1), jnp.int32),
        ),
        scratch_shapes=[pltpu.VMEM((32, 128), jnp.int32)],
        compiler_params=SMALL,
    )(layer.reshape(1), tok.reshape(1), segment_ids.reshape(16, 128))


def chunk_kernel(pieces, first, last, n_blocks, ids_ref, labels_ref, ta_ref, tg_ref, *refs):
    blocks, rest = refs[:n_blocks], refs[n_blocks:]
    trains = (ta_ref, tg_ref)
    width = 4 * BLOCK
    tile = 1024
    ids = jnp.concatenate(
        [ids_ref[r : r + 1, width * h : width * h + width] for r, h in pieces], 1
    )
    sel = (labels_ref[...] == ids).astype(F32).astype(BF16)
    nt = (((1,), (1,)), ((), ()))
    outs = rest if first else rest[1:]
    tiles = ta_ref.shape[1] // tile
    copies = {}
    if first:
        kept, sems = rest[1:3], rest[3]
        for j in range(tiles):
            for layer in range(2):
                for k in range(2):
                    piece = (layer, slice(j * tile, (j + 1) * tile))
                    copies[j, layer, k] = pltpu.make_async_copy(
                        trains[k].at[piece], kept[k].at[piece], sems.at[j, layer, k]
                    )
        for copy in copies.values():
            copy.start()
        trains = kept
    for j in range(tiles):
        cols = slice(j * tile, (j + 1) * tile)
        prods = []
        for layer in range(2):
            grams = []
            for k in range(2):
                if first:
                    copies[j, layer, k].wait()
                test = jnp.concatenate([b[:, k, layer].reshape(-1, 256) for b in blocks], 0)
                grams.append(
                    lax.dot_general(test, trains[k][layer, cols], nt, preferred_element_type=F32)
                )
            prods.append((grams[0] * grams[1]).astype(BF16))
        part = jnp.dot(
            jnp.concatenate([sel] * 2, 1), jnp.concatenate(prods, 0), preferred_element_type=F32
        )
        if not first:
            part = part + rest[0][:, cols]
        if last:
            outs[0][:, cols] = part[: Q // 2]
            outs[1][:, cols] = part[Q // 2 :].astype(BF16)
        else:
            outs[0][:, cols] = part


def chunk(pieces, blocks, acc, last, ids, labels, trains):
    first = acc is None
    rows = trains[0].shape[1]
    args = [ids, labels, *trains, *blocks] + ([] if first else [acc])
    if last:
        out_shape = (
            jax.ShapeDtypeStruct((Q // 2, rows), F32),
            jax.ShapeDtypeStruct((Q // 2, rows), BF16),
        )
    else:
        out_shape = (jax.ShapeDtypeStruct((Q, rows), F32),)
    if first:
        out_shape += tuple(jax.ShapeDtypeStruct(t.shape, t.dtype) for t in trains)
    s_rows = BLOCK * sum(b.shape[0] for b in blocks)
    return pl.pallas_call(
        functools.partial(chunk_kernel, pieces, first, last, len(blocks)),
        in_specs=[VMEM] * 2 + [HBM if first else VMEM] * 2 + [VMEM] * (len(args) - 4),
        out_specs=(VMEM,) * len(out_shape),
        out_shape=out_shape,
        scratch_shapes=[pltpu.SemaphoreType.DMA((rows // 1024, 2, 2))] if first else [],
        compiler_params=pltpu.CompilerParams(vmem_limit_bytes=(48 if first else 16) * 1024 * 1024),
        cost_estimate=pl.CostEstimate(
            flops=2 * 2 * s_rows * rows * (2 * 256 + Q),
            bytes_accessed=1024 * 1024,
            transcendentals=0,
        ),
    )(*args)


def merge_kernel(keep_ref, got_ref, own_ref, *send_refs):
    own_ref[...] = keep_ref[0:16] + got_ref[0:16].astype(F32)
    for k, ref in enumerate(send_refs, 1):
        rows = slice(16 * k, 16 * k + 16)
        ref[...] = (keep_ref[rows] + got_ref[rows].astype(F32)).astype(BF16)


def merge(keep, got):
    rows = keep.shape[1]
    part = jax.ShapeDtypeStruct((16, rows), BF16)
    return pl.pallas_call(
        merge_kernel,
        in_specs=[VMEM] * 2,
        out_specs=(VMEM,) * 4,
        out_shape=(jax.ShapeDtypeStruct((16, rows), F32), part, part, part),
        compiler_params=SMALL,
    )(keep, got)


def total_kernel(own_ref, *refs):
    total = own_ref[...]
    for ref in refs[:-1]:
        total = total + ref[...].astype(F32)
    refs[-1][...] = total


def total(own, parts):
    return pl.pallas_call(
        total_kernel,
        in_specs=[VMEM] * 4,
        out_specs=VMEM,
        out_shape=jax.ShapeDtypeStruct(own.shape, F32),
        compiler_params=SMALL,
    )(own, *parts)


def on_device(train_act, train_grad, test_act, test_grad, segment_ids):
    layer, tok = lax.axis_index("layer"), lax.axis_index("tok")
    sibling = moves(lambda h, c, x, z, y: (h, 1 - c, x, z, y))
    partner = moves(lambda h, c, x, z, y: (h, c, x, 1 - z, y))

    block = jnp.stack([test_act, test_grad])
    other = send(block, partner)
    trains = (train_act, train_grad)
    ids, labels = prepare(layer, tok, segment_ids)
    low = jnp.stack([block] + [send(block, other_way(d)) for d in (2, 1, -1)])
    other, ids, labels = lax.optimization_barrier((other, ids, labels))
    run = functools.partial(chunk, ids=ids, labels=labels, trains=trains)
    acc, *trains = run(((0, 0),), (low,), None, False)
    run = functools.partial(chunk, ids=ids, labels=labels, trains=trains)
    ring = [send(other, one_way(d)) for d in (-1, 1, 2)]
    ring, acc = lax.optimization_barrier((ring, acc))
    high = jnp.stack([other] + ring[::-1])

    low_prev, low_next = send(low, one_way(1)), send(low, one_way(-1))
    high_prev, high_next = send(high, other_way(1)), send(high, other_way(-1))
    low_far = (send(low_prev[:2], one_way(1)), send(low_next[2:], one_way(-1)))
    high_far = (send(high_prev[:2], other_way(1)), send(high_next[2:], other_way(-1)))
    (acc,) = run(((0, 1),), (high,), acc, False)
    (acc,) = run(((2, 0), (3, 0)), (low_prev, low_next), acc, False)
    high_prev, high_next, acc = lax.optimization_barrier((high_prev, high_next, acc))
    (acc,) = run(((2, 1), (3, 1)), (high_prev, high_next), acc, False)
    (acc,) = run(((1, 0),), low_far, acc, False)
    keep, give = run(((1, 1),), high_far, acc, True)

    own, *parts = merge(keep, send(give, sibling))
    parts = [send(parts[k - 1], along_z(k)) for k in (2, 1, 3)]
    return total(own, parts)


def solution(mesh):
    placed = (
        P("layer", "tok", None),
        P("layer", "tok", None),
        P("layer", "tok", None),
        P("layer", "tok", None),
        P(),
    )
    return jax.shard_map(
        on_device, mesh=mesh, in_specs=placed, out_specs=P("layer", "tok"), check_vma=False
    )
```

```python
import functools

import jax
import jax.numpy as jnp
from jax import lax
from jax.experimental import pallas as pl
from jax.experimental.pallas import tpu as pltpu
from jax.sharding import PartitionSpec as P

Q = 128
NX, NZ, NY = 4, 2, 4
NH, NC = 4, 2
BLOCK = 64
ORDER = (0, 2, 3, 1)
BF16 = jnp.bfloat16
F32 = jnp.float32
AXES = ("layer", "tok")
SMALL = pltpu.CompilerParams(vmem_limit_bytes=4 * 1024 * 1024)
HBM = pl.BlockSpec(memory_space=pltpu.HBM)
SMEM = pl.BlockSpec(memory_space=pltpu.SMEM)
VMEM = pl.BlockSpec(memory_space=pltpu.VMEM)


def moves(step):
    pairs = []
    for h in range(NH):
        for c in range(NC):
            for x in range(NX):
                for z in range(NZ):
                    for y in range(NY):
                        to = step(h, c, x, z, y)
                        here, there = (
                            (((i[0] % NH * NC + i[1] % NC) * NX + i[2] % NX) * NZ + i[3] % NZ) * NY
                            + i[4] % NY
                            for i in ((h, c, x, z, y), to)
                        )
                        pairs.append((here, there))
    return pairs


def one_way(d):
    return moves(lambda h, c, x, z, y: (h, c, x + d, z, y) if c == 1 else (h, c, x, z, y + d))


def other_way(d):
    return moves(lambda h, c, x, z, y: (h, c, x, z, y + d) if c == 1 else (h, c, x + d, z, y))


def along_z(d):
    return moves(lambda h, c, x, z, y: (h + d if c == 0 else h - d, c, x, z, y))


def send(value, pairs):
    return lax.ppermute(value, AXES, pairs)


def prepare_kernel(layer_ref, tok_ref, ids_ref, query_ref, label_ref, turned):
    core, z_hi = layer_ref[0] % 2, layer_ref[0] // 2
    x, z, y = tok_ref[0] // 8, tok_ref[0] // 4 % 2, tok_ref[0] % 4
    ids = ids_ref[...]
    turned[0:16] = ids
    turned[16:32] = pltpu.roll(ids, 64, 1)
    lane = lax.broadcasted_iota(jnp.int32, (1, 128), 1)
    for row, far in enumerate(ORDER):
        for half in range(2):
            for pair in range(2):
                got = []
                for n in range(2):
                    near = ORDER[2 * pair + n]
                    p, q = (far, near) if half == 0 else (near, far)
                    p, q = jnp.where(core == 1, p, q), jnp.where(core == 1, q, p)
                    tok = (x + p) % 4 * 8 + (z + half) % 2 * 4 + (y + q) % 4
                    turn = (tok + n) % 2
                    got.append(turned[pl.ds(turn * 16 + tok // 2, 1), :])
                at = 256 * half + 128 * pair
                query_ref[row : row + 1, at : at + 128] = jnp.where(lane < 64, got[0], got[1])
    r = lax.broadcasted_iota(jnp.int32, (Q, 1), 0)
    owner = jnp.where(r < 64, core, 1 - core)
    part = (r % 64) // 16
    label_ref[...] = (z_hi + jnp.where(owner == 0, part, 4 - part)) % 4 * 32 + owner * 16 + r % 16


def prepare(layer, tok, segment_ids):
    return pl.pallas_call(
        prepare_kernel,
        in_specs=[SMEM, SMEM, VMEM],
        out_specs=(VMEM, VMEM),
        out_shape=(
            jax.ShapeDtypeStruct((4, 2 * 4 * BLOCK), jnp.int32),
            jax.ShapeDtypeStruct((Q, 1), jnp.int32),
        ),
        scratch_shapes=[pltpu.VMEM((32, 128), jnp.int32)],
        compiler_params=SMALL,
    )(layer.reshape(1), tok.reshape(1), segment_ids.reshape(16, 128))


def chunk_kernel(pieces, first, last, n_blocks, ids_ref, labels_ref, ta_ref, tg_ref, *refs):
    blocks, rest = refs[:n_blocks], refs[n_blocks:]
    trains = (ta_ref, tg_ref)
    width = 4 * BLOCK
    tile = 1024
    ids = jnp.concatenate(
        [ids_ref[r : r + 1, width * h : width * h + width] for r, h in pieces], 1
    )
    sel = (labels_ref[...] == ids).astype(F32).astype(BF16)
    nt = (((1,), (1,)), ((), ()))
    outs = rest if first else rest[1:]
    tiles = ta_ref.shape[1] // tile
    copies = {}
    if first:
        kept, sems = rest[1:3], rest[3]
        for j in range(tiles):
            for layer in range(2):
                for k in range(2):
                    piece = (layer, slice(j * tile, (j + 1) * tile))
                    copies[j, layer, k] = pltpu.make_async_copy(
                        trains[k].at[piece], kept[k].at[piece], sems.at[j, layer, k]
                    )
        for copy in copies.values():
            copy.start()
        trains = kept
    for j in range(tiles):
        cols = slice(j * tile, (j + 1) * tile)
        prods = []
        for layer in range(2):
            grams = []
            for k in range(2):
                if first:
                    copies[j, layer, k].wait()
                test = jnp.concatenate([b[:, k, layer].reshape(-1, 256) for b in blocks], 0)
                grams.append(
                    lax.dot_general(test, trains[k][layer, cols], nt, preferred_element_type=F32)
                )
            prods.append((grams[0] * grams[1]).astype(BF16))
        part = jnp.dot(
            jnp.concatenate([sel] * 2, 1), jnp.concatenate(prods, 0), preferred_element_type=F32
        )
        if not first:
            part = part + rest[0][:, cols]
        if last:
            outs[0][:, cols] = part[: Q // 2]
            outs[1][:, cols] = part[Q // 2 :].astype(BF16)
        else:
            outs[0][:, cols] = part


def chunk(pieces, blocks, acc, last, ids, labels, trains):
    first = acc is None
    rows = trains[0].shape[1]
    args = [ids, labels, *trains, *blocks] + ([] if first else [acc])
    if last:
        out_shape = (
            jax.ShapeDtypeStruct((Q // 2, rows), F32),
            jax.ShapeDtypeStruct((Q // 2, rows), BF16),
        )
    else:
        out_shape = (jax.ShapeDtypeStruct((Q, rows), F32),)
    if first:
        out_shape += tuple(jax.ShapeDtypeStruct(t.shape, t.dtype) for t in trains)
    s_rows = BLOCK * sum(b.shape[0] for b in blocks)
    return pl.pallas_call(
        functools.partial(chunk_kernel, pieces, first, last, len(blocks)),
        in_specs=[VMEM] * 2 + [HBM if first else VMEM] * 2 + [VMEM] * (len(args) - 4),
        out_specs=(VMEM,) * len(out_shape),
        out_shape=out_shape,
        scratch_shapes=[pltpu.SemaphoreType.DMA((rows // 1024, 2, 2))] if first else [],
        compiler_params=pltpu.CompilerParams(vmem_limit_bytes=(48 if first else 16) * 1024 * 1024),
        cost_estimate=pl.CostEstimate(
            flops=2 * 2 * s_rows * rows * (2 * 256 + Q),
            bytes_accessed=1024 * 1024,
            transcendentals=0,
        ),
    )(*args)


def merge_kernel(keep_ref, got_ref, own_ref, *send_refs):
    own_ref[...] = keep_ref[0:16] + got_ref[0:16].astype(F32)
    for k, ref in enumerate(send_refs, 1):
        rows = slice(16 * k, 16 * k + 16)
        ref[...] = (keep_ref[rows] + got_ref[rows].astype(F32)).astype(BF16)


def merge(keep, got):
    rows = keep.shape[1]
    part = jax.ShapeDtypeStruct((16, rows), BF16)
    return pl.pallas_call(
        merge_kernel,
        in_specs=[VMEM] * 2,
        out_specs=(VMEM,) * 4,
        out_shape=(jax.ShapeDtypeStruct((16, rows), F32), part, part, part),
        compiler_params=SMALL,
    )(keep, got)


def total_kernel(own_ref, *refs):
    total = own_ref[...]
    for ref in refs[:-1]:
        total = total + ref[...].astype(F32)
    refs[-1][...] = total


def total(own, parts):
    return pl.pallas_call(
        total_kernel,
        in_specs=[VMEM] * 4,
        out_specs=VMEM,
        out_shape=jax.ShapeDtypeStruct(own.shape, F32),
        compiler_params=SMALL,
    )(own, *parts)


def on_device(train_act, train_grad, test_act, test_grad, segment_ids):
    layer, tok = lax.axis_index("layer"), lax.axis_index("tok")
    sibling = moves(lambda h, c, x, z, y: (h, 1 - c, x, z, y))
    partner = moves(lambda h, c, x, z, y: (h, c, x, 1 - z, y))

    block = jnp.stack([test_act, test_grad])
    other = send(block, partner)
    trains = (train_act, train_grad)
    ids, labels = prepare(layer, tok, segment_ids)
    low = jnp.stack([block] + [send(block, other_way(d)) for d in (2, 1, -1)])
    other, ids, labels = lax.optimization_barrier((other, ids, labels))
    run = functools.partial(chunk, ids=ids, labels=labels, trains=trains)
    acc, *trains = run(((0, 0),), (low,), None, False)
    run = functools.partial(chunk, ids=ids, labels=labels, trains=trains)
    ring = [send(other, one_way(d)) for d in (-1, 1, 2)]
    ring, acc = lax.optimization_barrier((ring, acc))
    high = jnp.stack([other] + ring[::-1])

    low_prev, low_next = send(low, one_way(1)), send(low, one_way(-1))
    high_prev, high_next = send(high, other_way(1)), send(high, other_way(-1))
    low_far = (send(low_prev[:2], one_way(1)), send(low_next[2:], one_way(-1)))
    high_far = (send(high_prev[:2], other_way(1)), send(high_next[2:], other_way(-1)))
    (acc,) = run(((0, 1),), (high,), acc, False)
    (acc,) = run(((2, 0), (3, 0)), (low_prev, low_next), acc, False)
    high_prev, high_next, acc = lax.optimization_barrier((high_prev, high_next, acc))
    (acc,) = run(((2, 1), (3, 1)), (high_prev, high_next), acc, False)
    (acc,) = run(((1, 0),), low_far, acc, False)
    keep, give = run(((1, 1),), high_far, acc, True)

    own, *parts = merge(keep, send(give, sibling))
    parts = [send(parts[k - 1], along_z(k)) for k in (2, 1, 3)]
    return total(own, parts)


def solution(mesh):
    placed = (
        P("layer", "tok", None),
        P("layer", "tok", None),
        P("layer", "tok", None),
        P("layer", "tok", None),
        P(),
    )
    return jax.shard_map(
        on_device, mesh=mesh, in_specs=placed, out_specs=P("layer", "tok"), check_vma=False
    )
```
